32 devices in a mesh: groups: 2 (over y), xy: 4 (over z), gz: 2 (over x), sub: 2 (over core).
Axes of the slice: x: 2, y: 2, z: 4, core: 2. Of those that a mesh axis runs over, the one named last changes fastest.
Arguments:
- top_plane: bfloat16 [128, 256, 128], P(('groups', 'xy'), ('sub', 'gz')), parts along dimension 0, may hold values from -6 to 6
- front_plane: bfloat16 [128, 32, 128], P(('groups', 'xy'), 'gz', 'sub'), parts along dimension 0, may hold values from -6 to 6
- side_plane: bfloat16 [512, 32, 128], P(('groups', 'sub'), 'gz', 'xy'), parts along dimension 0, may hold values from -6 to 6
- labels: int32 [128, 32, 256], P(('groups', 'xy'), 'gz', 'sub'), parts along dimension 0, may hold values from 0 to 17
- w_in: bfloat16 [128, 128], replicated, may hold values from -0.5 to 0.5
- b_in: float32 [128], replicated, may hold values from -3 to 3
- w_out: bfloat16 [128, 18], replicated, may hold values from -1.5 to 1.5
- b_out: float32 [18], replicated, may hold values from -3 to 3
Outputs:
- grad_top: float32 [128, 256, 128], P(('groups', 'xy'), ('sub', 'gz')), parts along dimension 0
- grad_front: float32 [128, 32, 128], P(('groups', 'xy'), 'gz', 'sub'), parts along dimension 0
- grad_side: float32 [512, 32, 128], P(('groups', 'sub'), 'gz', 'xy'), parts along dimension 0
- grad_w_in: float32 [256, 128], P('groups'), parts along dimension 0
- grad_b_in: float32 [256], P('groups'), parts along dimension 0
- grad_w_out: float32 [256, 18], P('groups'), parts along dimension 0
- grad_b_out: float32 [36], P('groups'), parts along dimension 0
The draws below stay inside these ranges and needn't reach their ends.
There are 2 independent parts, one for each index of `groups`. The reference program is written for one: setup_inputs(seed, part) draws one part's arguments, and reference() takes and returns one part's arrays. A program takes and returns all parts, laid end to end along the dimension named above; an argument that names none is the same for every part. Nothing has to cross between parts.
All inputs are finite; a program needn't handle non-finite values.
Results may differ from the reference program's by a relative error of at most 0.0026.
Values may be sent and summed in bfloat16 or wider, within the bound.
A program may use at most 64 MiB of HBM per device.

```python
import jax
import jax.numpy as jnp
from jax import lax

C = 128
H = 128
K = 18
X = 64
Y = 256
Z = 32
VOXELS = 524288


def place_ends(drawn, stream_key, smallest, high):
    longest = drawn.shape.index(max(drawn.shape))
    spots = []
    for shift in (0, 1):
        where = [jax.random.randint(jax.random.fold_in(stream_key, axis), (), 0, length) for axis, length in enumerate(drawn.shape)]
        where[longest] = (where[longest] + shift) % drawn.shape[longest]
        spots.append(tuple(where))
    return drawn.at[spots[0]].set(smallest).at[spots[1]].set(high)


def block_scale(rng, shape, cuts, low, top_value):
    loudness, own = 1.0, jax.random.fold_in(rng, 6)
    for position, parts in cuts:
        heights = jnp.exp(jax.random.uniform(jax.random.fold_in(own, position), (parts,), jnp.float32, low / len(cuts), top_value / len(cuts)))
        loudness = loudness * jnp.repeat(heights, shape[position] // parts).reshape([-1 if axis == position else 1 for axis in range(len(shape))])
    return loudness


def noise(own_key, dims, deviation, most, shards=(), held_as=jnp.bfloat16):
    result = jax.random.normal(own_key, dims, jnp.float32) * deviation
    if len(shards) > 0:
        result = block_scale(own_key, dims, shards, -0.22, 0.18) * result
    return jnp.clip(result, min=-most, max=most).astype(held_as)


def setup_inputs(seed: int = 0, part: int = 0) -> dict:
    key_of = jax.random.split(jax.random.key(seed), 9)
    part_splits = jax.random.split(jax.random.fold_in(key_of[8], part), 9)
    top_plane = noise(part_splits[0], (X, Y, C), 0.6, 6.0, ((0, 4), (1, 4)))
    front_plane = noise(part_splits[1], (X, Z, C), 0.6, 6.0, ((0, 4), (1, 2), (2, 2)))
    side_plane = noise(part_splits[2], (Y, Z, C), 0.6, 6.0, ((0, 2), (1, 2), (2, 4)))
    labels = place_ends(jax.random.randint(part_splits[3], (X, Z, Y), 0, K), jax.random.fold_in(part_splits[3], 1), 0, K - 1).astype(jnp.int32)
    w_in = noise(key_of[4], (C, H), C ** -0.5, 0.5)
    b_in = noise(key_of[5], (H,), 0.5, 3.0, (), jnp.float32)
    w_out = noise(key_of[6], (H, K), (H // 8) ** -0.5, 1.5)
    b_out = noise(key_of[7], (K,), 1.0, 3.0, (), jnp.float32)
    return {"top_plane": top_plane, "front_plane": front_plane, "side_plane": side_plane, "labels": labels, "w_in": w_in, "b_in": b_in, "w_out": w_out, "b_out": b_out}


def voxel_block(top_row, front_row, label_row, side_f, w_in, b_in, w_out, b_out):
    rows_y, rows_z, chans = side_f.shape
    feat = (top_row[:, None, :].astype(jnp.float32) + front_row[None, :, :].astype(jnp.float32) + side_f).astype(jnp.bfloat16).reshape(rows_y * rows_z, chans)
    pre = jnp.dot(feat, w_in, preferred_element_type=jnp.float32) + b_in
    sig = jax.nn.sigmoid(pre)
    hid = (pre * sig).astype(jnp.bfloat16)
    logits = jnp.dot(hid, w_out, preferred_element_type=jnp.float32) + b_out
    expo = jnp.exp(logits)
    prob = expo / jnp.sum(expo, axis=1, keepdims=True)
    classes = jnp.arange(w_out.shape[1], dtype=jnp.int32)
    onehot = (label_row.T.reshape(-1)[:, None] == classes[None, :]).astype(jnp.float32)
    dlog = (prob - onehot).astype(jnp.bfloat16)
    dhid = lax.dot_general(dlog, w_out, (((1,), (1,)), ((), ())), preferred_element_type=jnp.float32)
    dpre = (dhid * sig * (1.0 + pre * (1.0 - sig))).astype(jnp.bfloat16)
    dfeat = lax.dot_general(dpre, w_in, (((1,), (1,)), ((), ())), preferred_element_type=jnp.float32)
    gw1 = lax.dot_general(feat, dpre, (((0,), (0,)), ((), ())), preferred_element_type=jnp.float32)
    gb1 = jnp.sum(dpre.astype(jnp.float32), axis=0)
    gw2 = lax.dot_general(hid, dlog, (((0,), (0,)), ((), ())), preferred_element_type=jnp.float32)
    gb2 = jnp.sum(dlog.astype(jnp.float32), axis=0)
    return dfeat.reshape(rows_y, rows_z, chans), gw1, gb1, gw2, gb2


def reference(top_plane, front_plane, side_plane, labels, w_in, b_in, w_out, b_out):
    side_f = side_plane.astype(jnp.float32)

    def step(carry, inputs):
        side_acc, gw1, gb1, gw2, gb2 = carry
        top_row, front_row, label_row = inputs
        dgrid, a1, a2, a3, a4 = voxel_block(top_row, front_row, label_row, side_f, w_in, b_in, w_out, b_out)
        carry = (side_acc + dgrid, gw1 + a1, gb1 + a2, gw2 + a3, gb2 + a4)
        return carry, (jnp.sum(dgrid, axis=1), jnp.sum(dgrid, axis=0))

    init = (jnp.zeros(side_f.shape, jnp.float32), jnp.zeros(w_in.shape, jnp.float32), jnp.zeros(b_in.shape, jnp.float32), jnp.zeros(w_out.shape, jnp.float32), jnp.zeros(b_out.shape, jnp.float32))
    carry, outs = lax.scan(step, init, (top_plane, front_plane, labels))
    side_acc, gw1, gb1, gw2, gb2 = carry
    grad_top, grad_front = outs
    return grad_top, grad_front, side_acc, gw1 / VOXELS, gb1 / VOXELS, gw2 / VOXELS, gb2 / VOXELS
```

```python
import functools

import jax
import jax.numpy as jnp
from jax import lax
from jax.experimental import pallas as pl
from jax.experimental.pallas import tpu as pltpu
from jax.sharding import PartitionSpec as P

F32 = jnp.float32
BF16 = jnp.bfloat16
KP = 32
KU = 24
L = 128


def dot(a, b, ca=1, cb=0):
    return lax.dot_general(a, b, (((ca,), (cb,)), ((), ())), preferred_element_type=F32)


def split(v):
    hi = v.astype(BF16)
    return hi, (v - hi.astype(F32)).astype(BF16)


def exact_dot(v, w, cb):
    hi, lo = split(v)
    return dot(hi, w, 1, cb) + dot(lo, w, 1, cb)


def kernel(cfg, top_ref, front_ref, side_ref, lab_ref, w_ref, b_ref, wo_ref, bo_ref,
           otop_ref, ofront_ref, oside_ref, ogw_ref,
           top_all, front_all, side_all, e_side, e_front, wp, t_s, f_s, s_s, hid_s, g_s,
           a_top, a_front, a_side, a_gw2, a_gb2,
           top_snd, top_rcv, front_snd, front_rcv, side_snd, side_rcv,
           gw_loc, gw_sub, gw_gz, gw_part2, gw_xy, gw_half,
           sem_s, sem_r):
    ns, nx, ng, nb_, nch, yc, xs, zs, total = cfg
    nsub = nb_
    ix, ig, isub = lax.axis_index("xy"), lax.axis_index("gz"), lax.axis_index("sub")
    ids = {"xy": (ix, nx), "gz": (ig, ng), "sub": (isub, nsub)}
    r = L // yc
    nblk = zs // r
    qs = ns
    zq = zs // qs
    cs = L // ns
    cf = L // nsub

    def peer(axis, s):
        me, n = ids[axis]
        return lax.rem(me + s, n)

    def source(axis, s):
        me, n = ids[axis]
        return lax.rem(me + n - s, n)

    counter = [0]

    def remote(src, dst, axis, s):
        k = counter[0]
        counter[0] += 1
        return pltpu.make_async_remote_copy(
            src_ref=src, dst_ref=dst, send_sem=sem_s.at[k], recv_sem=sem_r.at[k],
            device_id={axis: peer(axis, s)}, device_id_type=pl.DeviceIdType.MESH)

    bar = pltpu.get_barrier_semaphore()
    greet = 0
    for axis in ("sub", "gz", "xy"):
        for s in range(1, ids[axis][1]):
            pl.semaphore_signal(bar, inc=1, device_id={axis: peer(axis, s)}, device_id_type=pl.DeviceIdType.MESH)
            greet += 1
    pl.semaphore_wait(bar, greet)

    started = []

    def go(copy):
        copy.start()
        started.append(copy)
        return copy

    side_cp = [[go(remote(side_ref.at[c], side_all.at[s - 1, c], "xy", s)) for s in range(1, ns)] for c in range(1)]
    top_cp = [go(remote(top_ref, top_all.at[s - 1], "gz", s)) for s in range(1, ng)]
    front_cp = [go(remote(front_ref, front_all.at[s - 1], "sub", s)) for s in range(1, nsub)]
    side_cp += [[go(remote(side_ref.at[c], side_all.at[s - 1, c], "xy", s)) for s in range(1, ns)] for c in range(1, nch)]

    w = w_ref[...]
    e_side[...] = jnp.zeros_like(e_side)
    for j in range(ns):
        for q in range(qs):
            e_side[j, q * cs:(q + 1) * cs, q * L:(q + 1) * L] = w[j * cs:(j + 1) * cs, :]
    e_front[...] = jnp.zeros_like(e_front)
    for j in range(nsub):
        for q in range(nsub):
            e_front[j, q * cf:(q + 1) * cf, q * L:(q + 1) * L] = w[j * cf:(j + 1) * cf, :]
    wp[...] = jnp.zeros_like(wp)
    wp[0:KP, 0:L] = wo_ref[...]
    wp[KP:2 * KP, L:2 * L] = wo_ref[...]
    a_side[...] = jnp.zeros_like(a_side)
    a_front[...] = jnp.zeros_like(a_front)
    a_gw2[...] = jnp.zeros_like(a_gw2)
    a_gb2[...] = jnp.zeros_like(a_gb2)

    yb = top_ref.shape[1]

    def project_top(plane, owner):
        v = (dot(plane.reshape(xs * yb, L), w) + b_ref[...]) * 0.5
        t_s[:, pl.ds(pl.multiple_of(owner * yb, yb), yb), :] = v.reshape(xs, yb, L)

    project_top(top_ref[...], ig)
    for s in range(1, ng):
        top_cp[s - 1].wait_recv()
        project_top(top_all[s - 1], source("gz", s))

    for cp in front_cp:
        cp.wait_recv()
    fp = dot(front_ref[...], e_front[isub])
    for s in range(1, nsub):
        fp = fp + dot(front_all[s - 1], e_front[source("sub", s)])
    fp = fp * 0.5
    frows = xs * zs // nsub
    for q in range(nsub):
        f_s[q * (xs // nsub):(q + 1) * (xs // nsub)] = fp[:, q * L:(q + 1) * L].reshape(xs // nsub, zs, L)

    iota_k = lax.broadcasted_iota(jnp.int32, (KU, L), 0)
    bo = bo_ref[0:KU, :]
    out_cp = []

    for c in range(nch):
        for cp in side_cp[c]:
            cp.wait_recv()
        sp = dot(side_ref[c], e_side[ix if ns > 1 else 0])
        for s in range(1, ns):
            sp = sp + dot(side_all[s - 1, c], e_side[source("xy", s)])
        sp = sp * 0.5
        bq = nblk // qs
        for q in range(qs):
            s_s[q * bq:(q + 1) * bq] = sp[:, q * L:(q + 1) * L].reshape(bq, L, L)

        def x_body(xi, _):
            t_x = t_s[xi, c * yc:(c + 1) * yc, :]
            t_blk = jnp.concatenate([t_x] * r, axis=0) if r > 1 else t_x
            f_x = f_s[xi]
            top_acc = jnp.zeros((yc, L), F32)
            gw2 = jnp.zeros((KP, L), F32)
            gb2 = jnp.zeros((KU, L), F32)
            for pair in range(nblk // 2):
                hs = []
                for i in range(2):
                    b = pair * 2 + i
                    if r > 1:
                        f_blk = jnp.concatenate(
                            [jnp.broadcast_to(f_x[b * r + k:b * r + k + 1], (yc, L)) for k in range(r)], axis=0)
                    else:
                        f_blk = f_x[b:b + 1]
                    p = t_blk + (s_s[b] + f_blk)
                    t = jnp.tanh(p)
                    u = 1.0 + t
                    hid = p * u
                    g_s[b] = (u + hid * (1.0 - t)).astype(BF16)
                    hs.append(hid.astype(BF16))
                h_cat = jnp.concatenate(hs, axis=1)
                logits = dot(wp[...], h_cat, 1, 1)
                dls = []
                for i in range(2):
                    b = pair * 2 + i
                    lg = logits[i * KP:i * KP + KU] + bo
                    ex = jnp.exp(lg - jnp.max(lg, axis=0, keepdims=True))
                    prob = ex * (1.0 / jnp.sum(ex, axis=0, keepdims=True))
                    lab = lab_ref[xi, c, b:b + 1, :]
                    dl = prob - jnp.where(iota_k == lab, 1.0, 0.0)
                    gb2 = gb2 + dl
                    dls.append(jnp.concatenate([dl, jnp.zeros((KP - KU, L), F32)], axis=0).astype(BF16))
                gw2 = gw2 + dot(jnp.concatenate(dls, axis=1), jnp.concatenate(hs, axis=0))
                dhid = dot(jnp.concatenate(dls, axis=0), wp[...], 0, 0)
                for i in range(2):
                    b = pair * 2 + i
                    dpre = dhid[:, i * L:(i + 1) * L] * g_s[b].astype(F32)
                    a_side[c, b] += dpre
                    for k in range(r):
                        part = dpre[k * yc:(k + 1) * yc]
                        top_acc = top_acc + part
                        z = b * r + k
                        a_front[xi, z:z + 1, :] += jnp.sum(part, axis=0, keepdims=True)
            a_top[xi, c * yc:(c + 1) * yc, :] = top_acc
            a_gw2[...] += gw2
            a_gb2[...] += gb2
            return 0

        lax.fori_loop(0, xs, x_body, 0)

        acc = a_side[c] * 0.5
        a_side[c] = acc
        cat = jnp.concatenate([acc[q * bq:(q + 1) * bq].reshape(bq * L, L) for q in range(qs)], axis=1)
        hi, lo = split(cat)
        for s in range(1, ns):
            e = e_side[peer("xy", s)]
            side_snd[s - 1, c] = (dot(hi, e, 1, 1) + dot(lo, e, 1, 1)).astype(BF16)
            out_cp.append((c, s, go(remote(side_snd.at[s - 1, c], side_rcv.at[s - 1, c], "xy", s))))
        e = e_side[ix if ns > 1 else 0]
        oside_ref[c] = dot(hi, e, 1, 1) + dot(lo, e, 1, 1)

    a_top[...] = a_top[...] * 0.5
    front_sum = a_front[...] * 0.5
    gw1 = jnp.zeros((L, L), F32)
    for s in range(ng):
        plane = top_ref[...] if s == 0 else top_all[s - 1]
        own = ig if s == 0 else source("gz", s)
        rows = a_top[:, pl.ds(pl.multiple_of(own * yb, yb), yb), :].reshape(xs * yb, L)
        gw1 = gw1 + dot(plane.reshape(xs * yb, L), rows.astype(BF16), 0, 0)
        if s > 0:
            top_snd[s - 1] = exact_dot(rows, w, 1).astype(BF16).reshape(xs, yb, L)
    for s in range(1, ng):
        go_cp = go(remote(top_snd.at[ng - s - 1], top_rcv.at[s - 1], "gz", s))
        out_cp.append(("top", s, go_cp))

    fcat = jnp.concatenate(
        [front_sum[q * (xs // nsub):(q + 1) * (xs // nsub)].reshape(frows, L) for q in range(nsub)], axis=1)
    fhi, flo = split(fcat)
    for s in range(1, nsub):
        e = e_front[peer("sub", s)]
        front_snd[s - 1] = dot(fhi, e, 1, 1) + dot(flo, e, 1, 1)
        out_cp.append(("front", s, go(remote(front_snd.at[s - 1], front_rcv.at[s - 1], "sub", s))))
    e = e_front[isub]
    ofront_ref[...] = dot(fhi, e, 1, 1) + dot(flo, e, 1, 1)

    for s in range(nsub):
        plane = front_ref[...] if s == 0 else front_all[s - 1]
        own = isub if s == 0 else source("sub", s)
        m = dot(plane, fhi, 0, 0)
        v = jnp.zeros((cf, L), F32)
        for q in range(nsub):
            v = v + m[q * cf:(q + 1) * cf, q * L:(q + 1) * L]
        gw_loc[pl.ds(pl.multiple_of(own * cf, cf), cf), :] = v
    gw_loc[0:L, :] = gw_loc[0:L, :] + gw1
    for s in range(ns):
        own = (ix if s == 0 else source("xy", s)) if ns > 1 else 0
        v = jnp.zeros((cs, L), F32)
        for c in range(nch):
            plane = side_ref[c] if s == 0 else side_all[s - 1, c]
            cat = jnp.concatenate(
                [a_side[c, q * bq:(q + 1) * bq].reshape(bq * L, L).astype(BF16) for q in range(qs)], axis=1)
            m = dot(plane, cat, 0, 0)
            for q in range(qs):
                v = v + m[q * cs:(q + 1) * cs, q * L:(q + 1) * L]
        at = pl.ds(pl.multiple_of(own * cs, cs), cs)
        gw_loc[at, :] = gw_loc[at, :] + v
    gw_loc[L:L + KU, :] = a_gw2[0:KU, :]
    gb1 = jnp.sum(front_sum.reshape(xs * zs, L), axis=0, keepdims=True)
    gb2 = jnp.sum(a_gb2[...], axis=1, keepdims=True)
    eye = (lax.broadcasted_iota(jnp.int32, (KU, L), 0) == lax.broadcasted_iota(jnp.int32, (KU, L), 1)).astype(F32)
    gb2_row = jnp.sum(gb2 * eye, axis=0, keepdims=True)
    gw_loc[L + KU:L + KU + 8, :] = jnp.concatenate([gb1, gb2_row, jnp.zeros((6, L), F32)], axis=0)

    hr = (L + KU + 8) // nsub

    def rows_of(i):
        return pl.ds(pl.multiple_of(i * hr, hr), hr)

    cps = [go(remote(gw_loc.at[rows_of(peer("sub", s))], gw_sub.at[s - 1], "sub", s)) for s in range(1, nsub)]
    part = gw_loc[rows_of(isub), :]
    for s in range(1, nsub):
        cps[s - 1].wait_recv()
        part = part + gw_sub[s - 1]
    gw_gz[ig] = part
    cps = [go(remote(gw_gz.at[ig], gw_gz.at[ig], "gz", s)) for s in range(1, ng)]
    own_rows = a_top[:, pl.ds(pl.multiple_of(ig * yb, yb), yb), :].reshape(xs * yb, L)
    otop_ref[...] = exact_dot(own_rows, w, 1).reshape(xs, yb, L)
    for cp in cps:
        cp.wait_recv()
    part = gw_gz[0]
    for j in range(1, ng):
        part = part + gw_gz[j]
    gw_part2[ix] = part * (1.0 / total)
    cps = [go(remote(gw_part2.at[ix], gw_part2.at[ix], "xy", s)) for s in range(1, nx)]
    for cp in cps:
        cp.wait_recv()
    full = gw_part2[0]
    for j in range(1, nx):
        full = full + gw_part2[j]
    ogw_ref[rows_of(isub), :] = full
    gw_half[...] = full
    cps = [go(remote(gw_half, gw_xy.at[s - 1], "sub", s)) for s in range(1, nsub)]
    for s in range(1, nsub):
        cps[s - 1].wait_recv()
        ogw_ref[rows_of(source("sub", s)), :] = gw_xy[s - 1]

    for kind, s, cp in out_cp:
        cp.wait_recv()
        if kind == "top":
            otop_ref[...] += top_rcv[s - 1].astype(F32)
        elif kind == "front":
            ofront_ref[...] += front_rcv[s - 1]
        else:
            oside_ref[kind] += side_rcv[s - 1, kind].astype(F32)
    for cp in started:
        cp.wait_send()


NCH = 1


def on_device(nx, ng, nsub, top, front, side, labels, w_in, b_in, w_out, b_out):
    xs, zs, ys = labels.shape
    total = xs * zs * ys * nx * ng * nsub
    k = w_out.shape[1]
    ns = nx if L // nx >= 16 else 1
    if ns == 1:
        side = lax.all_gather(side, "xy", axis=2, tiled=True)
    nch = NCH
    yc = ys // nch
    r = L // yc
    cs, cf = L // ns, L // nsub
    zq = zs // ns
    side_p = side.reshape(nch, yc, ns, zq, cs).transpose(0, 3, 1, 2, 4).reshape(nch, zq * yc, L)
    front_p = front.reshape(nsub, xs * zs // nsub, cf).transpose(1, 0, 2).reshape(xs * zs // nsub, L)
    lab = labels.reshape(xs, zs // r, r, nch, yc).transpose(0, 3, 1, 2, 4).reshape(xs, nch, zs // r, L)
    wo = jnp.zeros((KP, L), BF16).at[:k].set(w_out.T)
    bo = jnp.full((KP, L), -1e30, F32).at[:k].set(jnp.broadcast_to(b_out[:, None], (k, L)))
    yb = top.shape[1]
    fr, sr = front_p.shape[0], zq * yc
    gr = L + KU + 8
    nblk = zs // r
    copies = nch * (ns - 1) * 2 + (ng - 1) * 3 + (nsub - 1) * 4 + (nx - 1)
    cfg = (ns, nx, ng, nsub, nch, yc, xs, zs, total)
    vm = pl.BlockSpec(memory_space=pltpu.VMEM)
    V = pltpu.VMEM
    one = max(ns - 1, 1)
    otop, ofront, oside, ogw = pl.pallas_call(
        functools.partial(kernel, cfg),
        out_shape=(
            jax.ShapeDtypeStruct(top.shape, F32),
            jax.ShapeDtypeStruct((fr, L), F32),
            jax.ShapeDtypeStruct((nch, sr, L), F32),
            jax.ShapeDtypeStruct((gr, L), F32),
        ),
        in_specs=[vm] * 8,
        out_specs=(vm,) * 4,
        scratch_shapes=[
            V((ng - 1,) + top.shape, BF16), V((nsub - 1, fr, L), BF16), V((one, nch, sr, L), BF16),
            V((ns, L, ns * L), BF16), V((nsub, L, nsub * L), BF16), V((2 * KP, 2 * L), BF16),
            V((xs, ys, L), F32), V((xs, zs, L), F32), V((nblk, L, L), F32),
            V((8, L), F32), V((nblk, L, L), BF16),
            V((xs, ys, L), F32), V((xs, zs, L), F32), V((nch, nblk, L, L), F32),
            V((KP, L), F32), V((KU, L), F32),
            V((ng - 1,) + top.shape, BF16), V((ng - 1,) + top.shape, BF16),
            V((nsub - 1, fr, L), F32), V((nsub - 1, fr, L), F32),
            V((one, nch, sr, L), BF16), V((one, nch, sr, L), BF16),
            V((gr, L), F32), V((nsub - 1, gr // nsub, L), F32),
            V((ng, gr // nsub, L), F32), V((nx, gr // nsub, L), F32),
            V((nsub - 1, gr // nsub, L), F32), V((gr // nsub, L), F32),
            pltpu.SemaphoreType.DMA((copies,)), pltpu.SemaphoreType.DMA((copies,)),
        ],
        compiler_params=pltpu.CompilerParams(
            collective_id=0, has_side_effects=True, vmem_limit_bytes=48 * 1024 * 1024),
    )(top, front_p, side_p, lab, w_in, b_in.reshape(1, L), wo, bo)
    gfront = ofront.reshape(fr, nsub, cf).transpose(1, 0, 2).reshape(front.shape)
    gside = oside.reshape(nch, zq, yc, ns, cs).transpose(0, 2, 3, 1, 4).reshape(side.shape)
    if ns == 1:
        gside = lax.psum_scatter(gside, "xy", scatter_dimension=2, tiled=True)
    return (otop, gfront, gside, ogw[:L], ogw[L + KU], ogw[L:L + k].T, ogw[L + KU + 1, :k])


def solution(mesh):
    in_specs = (
        P(("groups", "xy"), ("sub", "gz"), None),
        P(("groups", "xy"), "gz", "sub"),
        P(("groups", "sub"), "gz", "xy"),
        P(("groups", "xy"), "gz", "sub"),
        P(),
        P(),
        P(),
        P(),
    )
    out_specs = (
        P(("groups", "xy"), ("sub", "gz"), None),
        P(("groups", "xy"), "gz", "sub"),
        P(("groups", "sub"), "gz", "xy"),
        P("groups", None),
        P("groups"),
        P("groups", None),
        P("groups"),
    )
    body = functools.partial(on_device, mesh.shape["xy"], mesh.shape["gz"], mesh.shape["sub"])
    return jax.shard_map(body, mesh=mesh, in_specs=in_specs, out_specs=out_specs, check_vma=False)
```

```python
import functools

import jax
import jax.numpy as jnp
from jax import lax
from jax.experimental import pallas as pl
from jax.experimental.pallas import tpu as pltpu
from jax.sharding import PartitionSpec as P

F32 = jnp.float32
BF16 = jnp.bfloat16
KP = 32
KU = 24
L = 128
CHUNKS = 2


def dot(a, b, ca=1, cb=0):
    return lax.dot_general(a, b, (((ca,), (cb,)), ((), ())), preferred_element_type=F32)


def split(v):
    hi = v.astype(BF16)
    return hi, (v - hi.astype(F32)).astype(BF16)


def kernel(cfg, top_ref, front_ref, side_ref, lab_ref, w_ref, b_ref, wo_ref, bo_ref,
           otop_ref, ofront_ref, oside_ref, ogw1_ref, ogw2_ref, ogb_ref,
           top_all, front_all, side_all, wp, wl, ww, t_s, f_s, s_s, hid_s, g_s, dl_s, g_side,
           a_top, a_front, a_side, a_gw2, a_gb2,
           top_snd, top_rcv, front_snd, front_rcv, side_snd, side_rcv,
           gw_loc, gw_sub, gw_gz, gw_xy, gw_full,
           sem_s, sem_r):
    ns, nx, ng, nsub, xs, zs, ys, k, total = cfg
    ix, ig, isub = lax.axis_index("xy"), lax.axis_index("gz"), lax.axis_index("sub")
    ids = {"xy": (ix, nx), "gz": (ig, ng), "sub": (isub, nsub)}
    cs, cf = L // ns, L // nsub
    zc = zs // CHUNKS
    pairs = zc // 2
    yb = top_ref.shape[1]

    def peer(axis, s):
        me, n = ids[axis]
        return lax.rem(me + s, n)

    def source(axis, s):
        me, n = ids[axis]
        return lax.rem(me + n - s, n)

    counter = [0]
    started = []

    def go(src, dst, axis, s):
        i = counter[0]
        counter[0] += 1
        copy = pltpu.make_async_remote_copy(
            src_ref=src, dst_ref=dst, send_sem=sem_s.at[i], recv_sem=sem_r.at[i],
            device_id={axis: peer(axis, s)}, device_id_type=pl.DeviceIdType.MESH)
        copy.start()
        started.append(copy)
        return copy

    bar = pltpu.get_barrier_semaphore()
    greet = 0
    for axis in ("sub", "gz", "xy"):
        for s in range(1, ids[axis][1]):
            pl.semaphore_signal(bar, inc=1, device_id={axis: peer(axis, s)}, device_id_type=pl.DeviceIdType.MESH)
            greet += 1
    pl.semaphore_wait(bar, greet)

    def channels(i):
        return pl.ds(pl.multiple_of(i * cs, cs), cs)

    def columns(i):
        return pl.ds(pl.multiple_of(i * cf, cf), cf)

    def rows_y(i):
        return pl.ds(pl.multiple_of(i * yb, yb), yb)

    def heights(c):
        return pl.ds(c * zc, zc)

    mine = ix if ns > 1 else 0

    def send_side(c):
        return [go(side_ref.at[heights(c)], side_all.at[heights(c), channels(ix), :], "xy", s)
                for s in range(1, ns)]

    side_cp = [send_side(0)]
    front_cp = [go(front_ref, front_all.at[s - 1], "sub", s) for s in range(1, nsub)]
    top_cp = [go(top_ref, top_all.at[s - 1], "gz", s) for s in range(1, ng)]
    side_cp += [send_side(c) for c in range(1, CHUNKS)]

    side_all[:, channels(mine), :] = side_ref[...]
    w = w_ref[...]
    ww[:, 0:L] = w
    ww[:, L:2 * L] = w
    wo = wo_ref[...]
    wp[...] = jnp.zeros_like(wp)
    wp[0:KP, 0:L] = wo
    wp[KP:2 * KP, L:2 * L] = wo
    wl[...] = wp[...].T
    a_side[...] = jnp.zeros_like(a_side)
    a_front[...] = jnp.zeros_like(a_front)
    a_top[...] = jnp.zeros_like(a_top)
    a_gw2[...] = jnp.zeros_like(a_gw2)
    a_gb2[...] = jnp.zeros_like(a_gb2)

    def project_top(plane, owner):
        v = (dot(plane.reshape(xs * yb, L), w) + b_ref[...]) * 0.5
        t_s[:, rows_y(owner), :] = v.reshape(xs, yb, L)

    project_top(top_ref[...], ig)
    for cp in front_cp:
        cp.wait_recv()
    fp = dot(front_ref[...], w_ref[columns(isub), :])
    for s in range(1, nsub):
        fp = fp + dot(front_all[s - 1], w_ref[columns(source("sub", s)), :])
    f_s[...] = (fp * 0.5).reshape(xs, zs, L)
    for s in range(1, ng):
        top_cp[s - 1].wait_recv()
        project_top(top_all[s - 1], source("gz", s))

    iota_k = lax.broadcasted_iota(jnp.int32, (KU, L), 0)
    bo = bo_ref[0:KU, :]
    side_out = []

    for c in range(CHUNKS):
        for cp in side_cp[c]:
            cp.wait_recv()
        for i in range(zc):
            s_s[i] = dot(side_all[c * zc + i], w, 0, 0) * 0.5

        def x_body(xi, _):
            t_x = t_s[xi]
            f_x = f_s[xi, c * zc:(c + 1) * zc, :]
            for z in range(zc):
                p = t_x + (s_s[z] + f_x[z:z + 1])
                t = jnp.tanh(p)
                u = 1.0 + t
                hid = p * u
                at = slice((z // 2) * ys, (z // 2 + 1) * ys), slice((z % 2) * L, (z % 2 + 1) * L)
                g_s[at] = (u + hid * (1.0 - t)).astype(BF16)
                hid_s[at] = hid.astype(BF16)
            logits = dot(hid_s[...], wl[...])
            gb2 = jnp.zeros((KU, L), F32)
            for j in range(pairs):
                lt = logits[j * ys:(j + 1) * ys].T
                for i in range(2):
                    lg = lt[i * KP:i * KP + KU] + bo
                    ex = jnp.exp(lg - jnp.max(lg, axis=0, keepdims=True))
                    prob = ex * (1.0 / jnp.sum(ex, axis=0, keepdims=True))
                    z = c * zc + j * 2 + i
                    dl = prob - jnp.where(iota_k == lab_ref[xi, z:z + 1, :], 1.0, 0.0)
                    gb2 = gb2 + dl
                    dl_s[i * KP:(i + 1) * KP, j * ys:(j + 1) * ys] = jnp.concatenate(
                        [dl, jnp.zeros((KP - KU, L), F32)], axis=0).astype(BF16)
            a_gb2[...] += gb2
            dhid = dot(dl_s[...], wp[...], 0, 0)
            a_gw2[...] += dot(dl_s[...], hid_s[...])
            top_acc = a_top[xi]
            for z in range(zc):
                at = slice((z // 2) * ys, (z // 2 + 1) * ys), slice((z % 2) * L, (z % 2 + 1) * L)
                dpre = dhid[at] * g_s[at].astype(F32)
                a_side[c * zc + z] += dpre
                top_acc = top_acc + dpre
                a_front[xi, c * zc + z:c * zc + z + 1, :] = jnp.sum(dpre, axis=0, keepdims=True)
            a_top[xi] = top_acc
            return 0

        lax.fori_loop(0, xs, x_body, 0)

        for i in range(zc):
            z = c * zc + i
            v = a_side[z] * 0.5
            hi, lo = split(v)
            g = dot(ww[...], jnp.concatenate([hi, lo], axis=1), 1, 1)
            side_snd[z] = g.astype(BF16)
            g_side[i] = g
            a_side[z] = v
        oside_ref[heights(c)] = g_side[:, channels(mine), :]
        for s in range(1, ns):
            side_out.append((c, s, go(side_snd.at[heights(c), channels(peer("xy", s)), :],
                                      side_rcv.at[s - 1, heights(c)], "xy", s)))

    top_out = []
    for s in range(1, ng):
        rows = a_top[:, rows_y(peer("gz", s)), :].reshape(xs * yb, L) * 0.5
        hi, lo = split(rows)
        top_snd[s - 1] = dot(jnp.concatenate([hi, lo], axis=1), ww[...], 1, 1).astype(BF16).reshape(xs, yb, L)
        top_out.append(go(top_snd.at[s - 1], top_rcv.at[s - 1], "gz", s))

    front_sum = a_front[...].reshape(xs * zs, L) * 0.5
    fhi, flo = split(front_sum)
    fcat = jnp.concatenate([fhi, flo], axis=1)
    front_out = []
    for s in range(1, nsub):
        front_snd[s - 1] = dot(fcat, ww[columns(peer("sub", s)), :], 1, 1)
        front_out.append(go(front_snd.at[s - 1], front_rcv.at[s - 1], "sub", s))

    gw1 = jnp.zeros((L, L), F32)
    for z in range(zs):
        gw1 = gw1 + dot(side_all[z], a_side[z].astype(BF16))
    for s in range(ng):
        plane = top_ref[...] if s == 0 else top_all[s - 1]
        own = ig if s == 0 else source("gz", s)
        rows = (a_top[:, rows_y(own), :] * 0.5).reshape(xs * yb, L).astype(BF16)
        gw1 = gw1 + dot(plane.reshape(xs * yb, L), rows, 0, 0)
    gw_loc[0:L, :] = gw1
    for s in range(nsub):
        plane = front_ref[...] if s == 0 else front_all[s - 1]
        at = columns(isub if s == 0 else source("sub", s))
        gw_loc[at, :] = gw_loc[at, :] + dot(plane, fhi, 0, 0)
    gw_loc[L:L + KU, :] = a_gw2[0:KU, 0:L] + a_gw2[KP:KP + KU, L:2 * L]
    gb1 = jnp.sum(front_sum, axis=0, keepdims=True)
    gb2 = jnp.sum(a_gb2[...], axis=1, keepdims=True)
    eye = (lax.broadcasted_iota(jnp.int32, (KU, L), 0) == lax.broadcasted_iota(jnp.int32, (KU, L), 1)).astype(F32)
    gb2_row = jnp.sum(gb2 * eye, axis=0, keepdims=True)
    gw_loc[L + KU:L + KU + 8, :] = jnp.concatenate([gb1, gb2_row, jnp.zeros((6, L), F32)], axis=0)

    hr = (L + KU + 8) // nsub

    def rows_of(i):
        return pl.ds(pl.multiple_of(i * hr, hr), hr)

    cps = [go(gw_loc.at[rows_of(peer("sub", s))], gw_sub.at[s - 1], "sub", s) for s in range(1, nsub)]
    part = gw_loc[rows_of(isub), :]
    for s in range(1, nsub):
        cps[s - 1].wait_recv()
        part = part + gw_sub[s - 1]
    gw_gz[ig] = part
    cps = [go(gw_gz.at[ig], gw_gz.at[ig], "gz", s) for s in range(1, ng)]
    hi, lo = split(a_top[:, rows_y(ig), :].reshape(xs * yb, L) * 0.5)
    otop_ref[...] = dot(jnp.concatenate([hi, lo], axis=1), ww[...], 1, 1).reshape(xs, yb, L)
    ofront_ref[...] = dot(fcat, ww[columns(isub), :], 1, 1)
    for cp in cps:
        cp.wait_recv()
    part = gw_gz[0]
    for j in range(1, ng):
        part = part + gw_gz[j]
    gw_xy[ix] = part * (1.0 / total)
    cps = [go(gw_xy.at[ix], gw_xy.at[ix], "xy", s) for s in range(1, nx)]
    for s in range(1, nsub):
        front_out[s - 1].wait_recv()
        ofront_ref[...] += front_rcv[s - 1]
    for s in range(1, ng):
        top_out[s - 1].wait_recv()
        otop_ref[...] += top_rcv[s - 1].astype(F32)
    for c, s, cp in side_out:
        cp.wait_recv()
        oside_ref[heights(c)] += side_rcv[s - 1, heights(c)].astype(F32)
    for cp in cps:
        cp.wait_recv()
    full = gw_xy[0]
    for j in range(1, nx):
        full = full + gw_xy[j]
    gw_full[rows_of(isub), :] = full
    cps = [go(gw_full.at[rows_of(isub)], gw_full.at[rows_of(isub)], "sub", s) for s in range(1, nsub)]
    for cp in cps:
        cp.wait_recv()
    ogw1_ref[...] = gw_full[0:L, :]
    ogw2_ref[...] = gw_full[L:L + k, :]
    ogb_ref[...] = gw_full[L + KU:L + KU + 8, :]
    for cp in started:
        cp.wait_send()


def on_device(nx, ng, nsub, top, front, side, labels, w_in, b_in, w_out, b_out):
    xs, zs, ys = labels.shape
    total = xs * zs * ys * nx * ng * nsub
    k = w_out.shape[1]
    ns = nx if L // nx >= 16 else 1
    if ns == 1:
        side = lax.all_gather(side, "xy", axis=2, tiled=True)
    cs, cf = L // ns, L // nsub
    wo = jnp.zeros((KP, L), BF16).at[:k].set(w_out.T)
    bo = jnp.full((KP, L), -1e30, F32).at[:k].set(jnp.broadcast_to(b_out[:, None], (k, L)))
    gr = L + KU + 8
    rows = zs // CHUNKS // 2 * ys
    copies = CHUNKS * (ns - 1) * 2 + (ng - 1) * 3 + (nsub - 1) * 4 + (nx - 1)
    cfg = (ns, nx, ng, nsub, xs, zs, ys, k, total)
    vm = pl.BlockSpec(memory_space=pltpu.VMEM)
    V = pltpu.VMEM
    one = max(ns - 1, 1)
    otop, ofront, oside, ogw1, ogw2, ogb = pl.pallas_call(
        functools.partial(kernel, cfg),
        out_shape=(
            jax.ShapeDtypeStruct(top.shape, F32),
            jax.ShapeDtypeStruct((xs * zs, cf), F32),
            jax.ShapeDtypeStruct((zs, cs, ys), F32),
            jax.ShapeDtypeStruct((L, L), F32),
            jax.ShapeDtypeStruct((k, L), F32),
            jax.ShapeDtypeStruct((8, L), F32),
        ),
        in_specs=[vm] * 8,
        out_specs=(vm,) * 6,
        scratch_shapes=[
            V((ng - 1,) + top.shape, BF16), V((nsub - 1, xs * zs, cf), BF16), V((zs, L, ys), BF16),
            V((2 * KP, 2 * L), BF16), V((2 * L, 2 * KP), BF16), V((L, 2 * L), BF16),
            V((xs, ys, L), F32), V((xs, zs, L), F32), V((zs // CHUNKS, ys, L), F32),
            V((rows, 2 * L), BF16), V((rows, 2 * L), BF16), V((2 * KP, rows), BF16),
            V((zs // CHUNKS, L, ys), F32),
            V((xs, ys, L), F32), V((xs, zs, L), F32), V((zs, ys, L), F32),
            V((2 * KP, 2 * L), F32), V((KU, L), F32),
            V((ng - 1,) + top.shape, BF16), V((ng - 1,) + top.shape, BF16),
            V((nsub - 1, xs * zs, cf), F32), V((nsub - 1, xs * zs, cf), F32),
            V((zs, L, ys), BF16), V((one, zs, cs, ys), BF16),
            V((gr, L), F32), V((nsub - 1, gr // nsub, L), F32),
            V((ng, gr // nsub, L), F32), V((nx, gr // nsub, L), F32), V((gr, L), F32),
            pltpu.SemaphoreType.DMA((copies,)), pltpu.SemaphoreType.DMA((copies,)),
        ],
        compiler_params=pltpu.CompilerParams(
            collective_id=0, has_side_effects=True, vmem_limit_bytes=48 * 1024 * 1024),
    )(top, front.reshape(xs * zs, cf), side.transpose(1, 2, 0), labels, w_in, b_in.reshape(1, L), wo, bo)
    gside = oside.transpose(2, 0, 1)
    if ns == 1:
        gside = lax.psum_scatter(gside, "xy", scatter_dimension=2, tiled=True)
    return (otop, ofront.reshape(front.shape), gside, ogw1, ogb[0], ogw2.T, ogb[1, :k])


def solution(mesh):
    in_specs = (
        P(("groups", "xy"), ("sub", "gz"), None),
        P(("groups", "xy"), "gz", "sub"),
        P(("groups", "sub"), "gz", "xy"),
        P(("groups", "xy"), "gz", "sub"),
        P(),
        P(),
        P(),
        P(),
    )
    out_specs = (
        P(("groups", "xy"), ("sub", "gz"), None),
        P(("groups", "xy"), "gz", "sub"),
        P(("groups", "sub"), "gz", "xy"),
        P("groups", None),
        P("groups"),
        P("groups", None),
        P("groups"),
    )
    body = functools.partial(on_device, mesh.shape["xy"], mesh.shape["gz"], mesh.shape["sub"])
    return jax.shard_map(body, mesh=mesh, in_specs=in_specs, out_specs=out_specs, check_vma=False)
```

```python
import functools

import jax
import jax.numpy as jnp
from jax import lax
from jax.experimental import pallas as pl
from jax.experimental.pallas import tpu as pltpu
from jax.sharding import PartitionSpec as P

F32 = jnp.float32
BF16 = jnp.bfloat16
KP = 32
KU = 24
L = 128
CHUNKS = 4
SEGMENTS = 4
UNROLL = 2


def dot(a, b, ca=1, cb=0):
    return lax.dot_general(a, b, (((ca,), (cb,)), ((), ())), preferred_element_type=F32)


def split(v):
    hi = v.astype(BF16)
    return hi, (v - hi.astype(F32)).astype(BF16)


def kernel(cfg, top_hbm, front_ref, side_ref, lab_hbm, w_ref, b_ref, wo_ref, bo_ref,
           otop_ref, ofront_ref, oside_ref, ogw1_ref, ogw2_ref, ogb1_ref, ogb2_ref,
           top_ref, lab_ref, top_all, front_all, side_all, wp, wl, ww, t_s, f_s, s_s, hid_s, g_s, dl_s, g_side,
           a_top, a_front, a_side, a_gw2, a_gb2,
           top_snd, top_rcv, front_snd, front_rcv, side_snd, side_rcv,
           gw_loc, gw_sub, gw_gz, gw_xy, gw_full,
           sem_s, sem_r, sem_l):
    ns, nx, ng, nsub, xs, zs, ys, k, total = cfg
    ix, ig, isub = lax.axis_index("xy"), lax.axis_index("gz"), lax.axis_index("sub")
    ids = {"xy": (ix, nx), "gz": (ig, ng), "sub": (isub, nsub)}
    cs, cf = L // ns, L // nsub
    zc = zs // CHUNKS
    pairs = zc // 2
    yb = top_ref.shape[1]
    xc = xs // SEGMENTS

    def peer(axis, s):
        me, n = ids[axis]
        return lax.rem(me + s, n)

    def source(axis, s):
        me, n = ids[axis]
        return lax.rem(me + n - s, n)

    counter = [0]
    started = []

    def go(src, dst, axis, s):
        i = counter[0]
        counter[0] += 1
        copy = pltpu.make_async_remote_copy(
            src_ref=src, dst_ref=dst, send_sem=sem_s.at[i], recv_sem=sem_r.at[i],
            device_id={axis: peer(axis, s)}, device_id_type=pl.DeviceIdType.MESH)
        copy.start()
        started.append(copy)
        return copy

    def local(src, dst, i):
        copy = pltpu.make_async_copy(src, dst, sem_l.at[i])
        copy.start()
        return copy

    def channels(i):
        return pl.ds(pl.multiple_of(i * cs, cs), cs)

    def columns(i):
        return pl.ds(pl.multiple_of(i * cf, cf), cf)

    def rows_y(i):
        return pl.ds(pl.multiple_of(i * yb, yb), yb)

    def heights(c):
        return pl.ds(c * zc, zc)

    mine = ix if ns > 1 else 0

    def run(g):
        return pl.ds(g * xc, xc)

    def send_side(c):
        return [go(side_ref.at[heights(c)], side_all.at[heights(c), channels(ix), :], "xy", s)
                for s in range(1, ns)]

    loc_top = local(top_hbm, top_ref, 0)
    loc_side = local(side_ref, side_all.at[:, channels(mine), :], 1)
    loc_lab = local(lab_hbm, lab_ref, 2)

    bar = pltpu.get_barrier_semaphore()
    greet = 0
    for axis in ("sub", "gz", "xy"):
        for s in range(1, ids[axis][1]):
            pl.semaphore_signal(bar, inc=1, device_id={axis: peer(axis, s)}, device_id_type=pl.DeviceIdType.MESH)
            greet += 1
    pl.semaphore_wait(bar, greet)

    side_cp = [send_side(0)]
    front_cp = [go(front_ref, front_all.at[s - 1], "sub", s) for s in range(1, nsub)]
    top_cp = [[go(top_hbm.at[run(g)], top_all.at[s - 1, run(g)], "gz", s) for s in range(1, ng)]
              for g in range(SEGMENTS)]
    side_cp += [send_side(c) for c in range(1, CHUNKS)]

    w = w_ref[...]
    ww[:, 0:L] = w
    ww[:, L:2 * L] = w
    wp[...] = jnp.zeros_like(wp)
    wp[0:k, 0:L] = wo_ref[...]
    wp[KP:KP + k, L:2 * L] = wo_ref[...]
    wl[...] = wp[...].T
    gw_loc[...] = jnp.zeros_like(gw_loc)
    a_side[...] = jnp.zeros_like(a_side)
    a_front[...] = jnp.zeros_like(a_front)
    a_top[...] = jnp.zeros_like(a_top)
    a_gw2[...] = jnp.zeros_like(a_gw2)
    a_gb2[...] = jnp.zeros_like(a_gb2)

    def project_top(plane, owner, g):
        v = (dot(plane.reshape(xc * yb, L), w) + b_ref[...]) * 0.5
        t_s[run(g), rows_y(owner), :] = v.reshape(xc, yb, L)

    loc_top.wait()
    for g in range(SEGMENTS):
        project_top(top_ref[run(g)], ig, g)
    for cp in front_cp:
        cp.wait_recv()
    fp = dot(front_ref[...], w_ref[columns(isub), :])
    for s in range(1, nsub):
        fp = fp + dot(front_all[s - 1], w_ref[columns(source("sub", s)), :])
    f_s[...] = (fp * 0.5).reshape(xs, zs, L)
    iota_k = lax.broadcasted_iota(jnp.int32, (KU, L), 0)
    eye = (iota_k == lax.broadcasted_iota(jnp.int32, (KU, L), 1)).astype(F32)
    bias = jnp.sum(eye * bo_ref[...], axis=1, keepdims=True)
    bo = jnp.where(iota_k < k, jnp.broadcast_to(bias, (KU, L)), -1e30)
    loc_side.wait()
    loc_lab.wait()
    top_out = []
    side_out = []

    hr = (L + KU + 8) // nsub

    def rows_of(i):
        return pl.ds(pl.multiple_of(i * hr, hr), hr)

    def finish_top(g):
        gw1 = jnp.zeros((L, L), F32)
        for s in list(range(1, ng)) + [0]:
            own = peer("gz", s)
            rows = a_top[run(g), rows_y(own), :].reshape(xc * yb, L) * 0.5
            hi, lo = split(rows)
            v = dot(jnp.concatenate([hi, lo], axis=1), ww[...], 1, 1).reshape(xc, yb, L)
            if s > 0:
                top_snd[s - 1, run(g)] = v.astype(BF16)
                top_out.append((g, s, go(top_snd.at[s - 1, run(g)], top_rcv.at[s - 1, run(g)], "gz", s)))
                plane = top_all[ng - s - 1, run(g)]
            else:
                otop_ref[run(g)] = v
                plane = top_ref[run(g)]
            gw1 = gw1 + dot(plane.reshape(xc * yb, L), hi, 0, 0)
        gw_loc[0:L, :] += gw1

    gw_sub_cp = []

    def start_weights():
        front_sum = a_front[...].reshape(xs * zs, L) * 0.5
        fhi = front_sum.astype(BF16)
        gw1 = jnp.zeros((L, L), F32)
        for z in range(zs):
            gw1 = gw1 + dot(side_all[z], (a_side[z] * 0.5).astype(BF16))
        gw_loc[0:L, :] += gw1
        for s in range(nsub):
            plane = front_ref[...] if s == 0 else front_all[s - 1]
            at = columns(isub if s == 0 else source("sub", s))
            gw_loc[at, :] = gw_loc[at, :] + dot(plane, fhi, 0, 0)
        gw_loc[L:L + KU, :] = a_gw2[0:KU, 0:L] + a_gw2[KP:KP + KU, L:2 * L]
        gb1 = jnp.sum(front_sum, axis=0, keepdims=True)
        gb2 = jnp.sum(a_gb2[...], axis=1, keepdims=True)
        gb2_row = jnp.sum(gb2 * eye, axis=0, keepdims=True)
        gw_loc[L + KU:L + KU + 8, :] = jnp.concatenate([gb1, gb2_row, jnp.zeros((6, L), F32)], axis=0)
        gw_sub_cp.extend(go(gw_loc.at[rows_of(peer("sub", s))], gw_sub.at[s - 1], "sub", s) for s in range(1, nsub))
        part = gw_loc[rows_of(isub), :]
        for s in range(1, nsub):
            gw_sub_cp[s - 1].wait_recv()
            part = part + gw_sub[s - 1]
        gw_gz[ig] = part
        gw_gz_cp.extend(go(gw_gz.at[ig], gw_gz.at[ig], "gz", s) for s in range(1, ng))

    gw_gz_cp = []

    for c in range(CHUNKS):
        for cp in side_cp[c]:
            cp.wait_recv()
        for i in range(zc):
            s_s[i] = dot(side_all[c * zc + i], w, 0, 0) * 0.5

        def x_body(xi, _):
            t_x = t_s[xi]
            f_x = f_s[xi, c * zc:(c + 1) * zc, :]
            for z in range(zc):
                p = t_x + (s_s[z] + f_x[z:z + 1])
                t = jnp.tanh(p)
                u = 1.0 + t
                hid = p * u
                at = slice((z // 2) * ys, (z // 2 + 1) * ys), slice((z % 2) * L, (z % 2 + 1) * L)
                g_s[at] = (u + hid * (1.0 - t)).astype(BF16)
                hid_s[at] = hid.astype(BF16)
            logits = dot(hid_s[...], wl[...])
            gb2 = jnp.zeros((KU, L), F32)
            for j in range(pairs):
                lt = logits[j * ys:(j + 1) * ys].T
                for i in range(2):
                    lg = lt[i * KP:i * KP + KU] + bo
                    ex = jnp.exp(lg - jnp.max(lg, axis=0, keepdims=True))
                    prob = ex * (1.0 / jnp.sum(ex, axis=0, keepdims=True))
                    z = c * zc + j * 2 + i
                    dl = prob - jnp.where(iota_k == lab_ref[xi, z:z + 1, :], 1.0, 0.0)
                    gb2 = gb2 + dl
                    dl_s[i * KP:(i + 1) * KP, j * ys:(j + 1) * ys] = jnp.concatenate(
                        [dl, jnp.zeros((KP - KU, L), F32)], axis=0).astype(BF16)
            a_gb2[...] += gb2
            dhid = dot(dl_s[...], wp[...], 0, 0)
            a_gw2[...] += dot(dl_s[...], hid_s[...])
            top_acc = a_top[xi]
            for z in range(zc):
                at = slice((z // 2) * ys, (z // 2 + 1) * ys), slice((z % 2) * L, (z % 2 + 1) * L)
                dpre = dhid[at] * g_s[at].astype(F32)
                a_side[c * zc + z] += dpre
                top_acc = top_acc + dpre
                a_front[xi, c * zc + z:c * zc + z + 1, :] = jnp.sum(dpre, axis=0, keepdims=True)
            a_top[xi] = top_acc
            return 0

        if c == 0 or c == CHUNKS - 1:
            for g in range(SEGMENTS):
                if c == 0:
                    for s in range(1, ng):
                        top_cp[g][s - 1].wait_recv()
                        project_top(top_all[s - 1, run(g)], source("gz", s), g)
                lax.fori_loop(g * xc, (g + 1) * xc, x_body, 0, unroll=UNROLL)
                if c == CHUNKS - 1:
                    finish_top(g)
        else:
            lax.fori_loop(0, xs, x_body, 0, unroll=UNROLL)
        if c == CHUNKS - 1:
            start_weights()

        for i in range(zc):
            z = c * zc + i
            hi, lo = split(a_side[z] * 0.5)
            g = dot(ww[...], jnp.concatenate([hi, lo], axis=1), 1, 1)
            side_snd[z] = g.astype(BF16)
            g_side[i] = g
        oside_ref[heights(c)] = g_side[:, channels(mine), :]
        for s in range(1, ns):
            side_out.append((c, s, go(side_snd.at[heights(c), channels(peer("xy", s)), :],
                                      side_rcv.at[s - 1, heights(c)], "xy", s)))

    fcat = jnp.concatenate(split(a_front[...].reshape(xs * zs, L) * 0.5), axis=1)
    front_out = []
    for s in range(1, nsub):
        front_snd[s - 1] = dot(fcat, ww[columns(peer("sub", s)), :], 1, 1)
        front_out.append(go(front_snd.at[s - 1], front_rcv.at[s - 1], "sub", s))
    ofront_ref[...] = dot(fcat, ww[columns(isub), :], 1, 1)
    for cp in gw_gz_cp:
        cp.wait_recv()
    part = gw_gz[0]
    for j in range(1, ng):
        part = part + gw_gz[j]
    gw_xy[ix] = part * (1.0 / total)
    cps = [go(gw_xy.at[ix], gw_xy.at[ix], "xy", s) for s in range(1, nx)]
    for s in range(1, nsub):
        front_out[s - 1].wait_recv()
        ofront_ref[...] += front_rcv[s - 1]
    for g, s, cp in top_out:
        cp.wait_recv()
        otop_ref[run(g)] += top_rcv[s - 1, run(g)].astype(F32)
    for c, s, cp in side_out:
        cp.wait_recv()
        oside_ref[heights(c)] += side_rcv[s - 1, heights(c)].astype(F32)
    for cp in cps:
        cp.wait_recv()
    full = gw_xy[0]
    for j in range(1, nx):
        full = full + gw_xy[j]
    gw_full[rows_of(isub), :] = full
    cps = [go(gw_full.at[rows_of(isub)], gw_full.at[rows_of(isub)], "sub", s) for s in range(1, nsub)]
    for cp in cps:
        cp.wait_recv()
    ogw1_ref[...] = gw_full[0:L, :]
    ogw2_ref[...] = gw_full[L:L + k, :]
    ogb1_ref[...] = gw_full[L + KU:L + KU + 1, :]
    ogb2_ref[...] = gw_full[L + KU + 1:L + KU + 2, 0:k]
    for cp in started:
        cp.wait_send()


def store(*refs):
    sems = refs[-1]
    n = (len(refs) - 1) // 2
    copies = [pltpu.make_async_copy(refs[i], refs[n + i], sems.at[i]) for i in range(n)]
    for copy in copies:
        copy.start()
    for copy in copies:
        copy.wait()


def on_device(nx, ng, nsub, top, front, side, labels, w_in, b_in, w_out, b_out):
    xs, zs, ys = labels.shape
    total = xs * zs * ys * nx * ng * nsub
    k = w_out.shape[1]
    ns = nx if L // nx >= 16 else 1
    if ns == 1:
        side = lax.all_gather(side, "xy", axis=2, tiled=True)
    cs, cf = L // ns, L // nsub
    bo = jnp.pad(b_out, (0, L - k)).reshape(1, L)
    gr = L + KU + 8
    rows = zs // CHUNKS // 2 * ys
    copies = CHUNKS * (ns - 1) * 2 + (ng - 1) * (2 * SEGMENTS + 1) + (nsub - 1) * 4 + (nx - 1)
    cfg = (ns, nx, ng, nsub, xs, zs, ys, k, total)
    vm = pl.BlockSpec(memory_space=pltpu.VMEM)
    hbm = pl.BlockSpec(memory_space=pl.ANY)
    V = pltpu.VMEM
    one = max(ns - 1, 1)
    outs = pl.pallas_call(
        functools.partial(kernel, cfg),
        out_shape=(
            jax.ShapeDtypeStruct(top.shape, F32),
            jax.ShapeDtypeStruct((xs * zs, cf), F32),
            jax.ShapeDtypeStruct((zs, cs, ys), F32),
            jax.ShapeDtypeStruct((L, L), F32),
            jax.ShapeDtypeStruct((k, L), F32),
            jax.ShapeDtypeStruct((1, L), F32),
            jax.ShapeDtypeStruct((1, k), F32),
        ),
        in_specs=[hbm, vm, hbm, hbm, vm, vm, vm, vm],
        out_specs=(vm,) * 7,
        scratch_shapes=[
            V(top.shape, BF16), V(labels.shape, jnp.int32),
            V((ng - 1,) + top.shape, BF16), V((nsub - 1, xs * zs, cf), BF16), V((zs, L, ys), BF16),
            V((2 * KP, 2 * L), BF16), V((2 * L, 2 * KP), BF16), V((L, 2 * L), BF16),
            V((xs, ys, L), F32), V((xs, zs, L), F32), V((zs // CHUNKS, ys, L), F32),
            V((rows, 2 * L), BF16), V((rows, 2 * L), BF16), V((2 * KP, rows), BF16),
            V((zs // CHUNKS, L, ys), F32),
            V((xs, ys, L), F32), V((xs, zs, L), F32), V((zs, ys, L), F32),
            V((2 * KP, 2 * L), F32), V((KU, L), F32),
            V((ng - 1,) + top.shape, BF16), V((ng - 1,) + top.shape, BF16),
            V((nsub - 1, xs * zs, cf), F32), V((nsub - 1, xs * zs, cf), F32),
            V((zs, L, ys), BF16), V((one, zs, cs, ys), BF16),
            V((gr, L), F32), V((nsub - 1, gr // nsub, L), F32),
            V((ng, gr // nsub, L), F32), V((nx, gr // nsub, L), F32), V((gr, L), F32),
            pltpu.SemaphoreType.DMA((copies,)), pltpu.SemaphoreType.DMA((copies,)),
            pltpu.SemaphoreType.DMA((3,)),
        ],
        compiler_params=pltpu.CompilerParams(
            collective_id=0, has_side_effects=True, vmem_limit_bytes=48 * 1024 * 1024),
    )(top, front.reshape(xs * zs, cf), side.transpose(1, 2, 0), labels, w_in, b_in.reshape(1, L), w_out.T, bo)
    otop, ofront, oside, ogw1, ogw2, ogb1, ogb2 = pl.pallas_call(
        store,
        out_shape=tuple(jax.ShapeDtypeStruct(o.shape, F32) for o in outs),
        in_specs=[vm] * 7,
        out_specs=(hbm,) * 7,
        scratch_shapes=[pltpu.SemaphoreType.DMA((7,))],
    )(*outs)
    gside = oside.transpose(2, 0, 1)
    if ns == 1:
        gside = lax.psum_scatter(gside, "xy", scatter_dimension=2, tiled=True)
    return (otop, ofront.reshape(front.shape), gside, ogw1, ogb1[0], ogw2.T, ogb2[0])


def solution(mesh):
    in_specs = (
        P(("groups", "xy"), ("sub", "gz"), None),
        P(("groups", "xy"), "gz", "sub"),
        P(("groups", "sub"), "gz", "xy"),
        P(("groups", "xy"), "gz", "sub"),
        P(),
        P(),
        P(),
        P(),
    )
    out_specs = (
        P(("groups", "xy"), ("sub", "gz"), None),
        P(("groups", "xy"), "gz", "sub"),
        P(("groups", "sub"), "gz", "xy"),
        P("groups", None),
        P("groups"),
        P("groups", None),
        P("groups"),
    )
    body = functools.partial(on_device, mesh.shape["xy"], mesh.shape["gz"], mesh.shape["sub"])
    return jax.shard_map(body, mesh=mesh, in_specs=in_specs, out_specs=out_specs, check_vma=False)
```

```python
import functools

import jax
import jax.numpy as jnp
from jax import lax
from jax.experimental import pallas as pl
from jax.experimental.pallas import tpu as pltpu
from jax.sharding import PartitionSpec as P

F32 = jnp.float32
BF16 = jnp.bfloat16
KP = 32
KU = 24
L = 128
CHUNKS = 2


def dot(a, b, ca=1, cb=0):
    return lax.dot_general(a, b, (((ca,), (cb,)), ((), ())), preferred_element_type=F32)


def split(v):
    hi = v.astype(BF16)
    return hi, (v - hi.astype(F32)).astype(BF16)


def kernel(cfg, top_ref, front_ref, side_ref, lab_ref, w_ref, b_ref, wo_ref, bo_ref,
           otop_ref, ofront_ref, oside_ref, ogw1_ref, ogw2_ref, ogb_ref,
           top_all, front_all, side_all, wp, wl, ww, t_s, f_s, s_s, hid_s, g_s, dl_s, g_side,
           a_top, a_front, a_side, a_gw2, a_gb2,
           top_snd, top_rcv, front_snd, front_rcv, side_snd, side_rcv,
           gw_loc, gw_sub, gw_gz, gw_xy, gw_full,
           sem_s, sem_r):
    ns, nx, ng, nsub, xs, zs, ys, k, total = cfg
    ix, ig, isub = lax.axis_index("xy"), lax.axis_index("gz"), lax.axis_index("sub")
    ids = {"xy": (ix, nx), "gz": (ig, ng), "sub": (isub, nsub)}
    cs, cf = L // ns, L // nsub
    zc = zs // CHUNKS
    pairs = zc // 2
    yb = top_ref.shape[1]

    def peer(axis, s):
        me, n = ids[axis]
        return lax.rem(me + s, n)

    def source(axis, s):
        me, n = ids[axis]
        return lax.rem(me + n - s, n)

    counter = [0]
    started = []

    def go(src, dst, axis, s):
        i = counter[0]
        counter[0] += 1
        copy = pltpu.make_async_remote_copy(
            src_ref=src, dst_ref=dst, send_sem=sem_s.at[i], recv_sem=sem_r.at[i],
            device_id={axis: peer(axis, s)}, device_id_type=pl.DeviceIdType.MESH)
        copy.start()
        started.append(copy)
        return copy

    bar = pltpu.get_barrier_semaphore()
    greet = 0
    for axis in ("sub", "gz", "xy"):
        for s in range(1, ids[axis][1]):
            pl.semaphore_signal(bar, inc=1, device_id={axis: peer(axis, s)}, device_id_type=pl.DeviceIdType.MESH)
            greet += 1
    pl.semaphore_wait(bar, greet)

    def channels(i):
        return pl.ds(pl.multiple_of(i * cs, cs), cs)

    def columns(i):
        return pl.ds(pl.multiple_of(i * cf, cf), cf)

    def rows_y(i):
        return pl.ds(pl.multiple_of(i * yb, yb), yb)

    def heights(c):
        return pl.ds(c * zc, zc)

    mine = ix if ns > 1 else 0

    def send_side(c):
        return [go(side_ref.at[heights(c)], side_all.at[heights(c), channels(ix), :], "xy", s)
                for s in range(1, ns)]

    side_cp = [send_side(0)]
    front_cp = [go(front_ref, front_all.at[s - 1], "sub", s) for s in range(1, nsub)]
    top_cp = [go(top_ref, top_all.at[s - 1], "gz", s) for s in range(1, ng)]
    side_cp += [send_side(c) for c in range(1, CHUNKS)]

    side_all[:, channels(mine), :] = side_ref[...]
    w = w_ref[...]
    ww[:, 0:L] = w
    ww[:, L:2 * L] = w
    wp[...] = jnp.zeros_like(wp)
    wp[0:k, 0:L] = wo_ref[...]
    wp[KP:KP + k, L:2 * L] = wo_ref[...]
    wl[...] = wp[...].T
    a_side[...] = jnp.zeros_like(a_side)
    a_front[...] = jnp.zeros_like(a_front)
    a_top[...] = jnp.zeros_like(a_top)
    a_gw2[...] = jnp.zeros_like(a_gw2)
    a_gb2[...] = jnp.zeros_like(a_gb2)

    def project_top(plane, owner):
        v = (dot(plane.reshape(xs * yb, L), w) + b_ref[...]) * 0.5
        t_s[:, rows_y(owner), :] = v.reshape(xs, yb, L)

    project_top(top_ref[...], ig)
    for cp in front_cp:
        cp.wait_recv()
    fp = dot(front_ref[...], w_ref[columns(isub), :])
    for s in range(1, nsub):
        fp = fp + dot(front_all[s - 1], w_ref[columns(source("sub", s)), :])
    f_s[...] = (fp * 0.5).reshape(xs, zs, L)
    for s in range(1, ng):
        top_cp[s - 1].wait_recv()
        project_top(top_all[s - 1], source("gz", s))

    iota_k = lax.broadcasted_iota(jnp.int32, (KU, L), 0)
    eye = (iota_k == lax.broadcasted_iota(jnp.int32, (KU, L), 1)).astype(F32)
    bias = jnp.sum(eye * bo_ref[...], axis=1, keepdims=True)
    bo = jnp.where(iota_k < k, jnp.broadcast_to(bias, (KU, L)), -1e30)
    side_out = []

    for c in range(CHUNKS):
        for cp in side_cp[c]:
            cp.wait_recv()
        for i in range(zc):
            s_s[i] = dot(side_all[c * zc + i], w, 0, 0) * 0.5

        def x_body(xi, _):
            t_x = t_s[xi]
            f_x = f_s[xi, c * zc:(c + 1) * zc, :]
            for z in range(zc):
                p = t_x + (s_s[z] + f_x[z:z + 1])
                t = jnp.tanh(p)
                u = 1.0 + t
                hid = p * u
                at = slice((z // 2) * ys, (z // 2 + 1) * ys), slice((z % 2) * L, (z % 2 + 1) * L)
                g_s[at] = (u + hid * (1.0 - t)).astype(BF16)
                hid_s[at] = hid.astype(BF16)
            logits = dot(hid_s[...], wl[...])
            gb2 = jnp.zeros((KU, L), F32)
            for j in range(pairs):
                lt = logits[j * ys:(j + 1) * ys].T
                for i in range(2):
                    lg = lt[i * KP:i * KP + KU] + bo
                    ex = jnp.exp(lg - jnp.max(lg, axis=0, keepdims=True))
                    prob = ex * (1.0 / jnp.sum(ex, axis=0, keepdims=True))
                    z = c * zc + j * 2 + i
                    dl = prob - jnp.where(iota_k == lab_ref[xi, z:z + 1, :], 1.0, 0.0)
                    gb2 = gb2 + dl
                    dl_s[i * KP:(i + 1) * KP, j * ys:(j + 1) * ys] = jnp.concatenate(
                        [dl, jnp.zeros((KP - KU, L), F32)], axis=0).astype(BF16)
            a_gb2[...] += gb2
            dhid = dot(dl_s[...], wp[...], 0, 0)
            a_gw2[...] += dot(dl_s[...], hid_s[...])
            top_acc = a_top[xi]
            for z in range(zc):
                at = slice((z // 2) * ys, (z // 2 + 1) * ys), slice((z % 2) * L, (z % 2 + 1) * L)
                dpre = dhid[at] * g_s[at].astype(F32)
                a_side[c * zc + z] += dpre
                top_acc = top_acc + dpre
                a_front[xi, c * zc + z:c * zc + z + 1, :] = jnp.sum(dpre, axis=0, keepdims=True)
            a_top[xi] = top_acc
            return 0

        lax.fori_loop(0, xs, x_body, 0, unroll=2)

        for i in range(zc):
            z = c * zc + i
            v = a_side[z] * 0.5
            hi, lo = split(v)
            g = dot(ww[...], jnp.concatenate([hi, lo], axis=1), 1, 1)
            side_snd[z] = g.astype(BF16)
            g_side[i] = g
            a_side[z] = v
        oside_ref[heights(c)] = g_side[:, channels(mine), :]
        for s in range(1, ns):
            side_out.append((c, s, go(side_snd.at[heights(c), channels(peer("xy", s)), :],
                                      side_rcv.at[s - 1, heights(c)], "xy", s)))

    top_out = []
    for s in range(1, ng):
        rows = a_top[:, rows_y(peer("gz", s)), :].reshape(xs * yb, L) * 0.5
        hi, lo = split(rows)
        top_snd[s - 1] = dot(jnp.concatenate([hi, lo], axis=1), ww[...], 1, 1).astype(BF16).reshape(xs, yb, L)
        top_out.append(go(top_snd.at[s - 1], top_rcv.at[s - 1], "gz", s))

    front_sum = a_front[...].reshape(xs * zs, L) * 0.5
    fhi, flo = split(front_sum)
    fcat = jnp.concatenate([fhi, flo], axis=1)
    front_out = []
    for s in range(1, nsub):
        front_snd[s - 1] = dot(fcat, ww[columns(peer("sub", s)), :], 1, 1)
        front_out.append(go(front_snd.at[s - 1], front_rcv.at[s - 1], "sub", s))

    gw1 = jnp.zeros((L, L), F32)
    for z in range(zs):
        gw1 = gw1 + dot(side_all[z], a_side[z].astype(BF16))
    for s in range(ng):
        plane = top_ref[...] if s == 0 else top_all[s - 1]
        own = ig if s == 0 else source("gz", s)
        rows = (a_top[:, rows_y(own), :] * 0.5).reshape(xs * yb, L).astype(BF16)
        gw1 = gw1 + dot(plane.reshape(xs * yb, L), rows, 0, 0)
    gw_loc[0:L, :] = gw1
    for s in range(nsub):
        plane = front_ref[...] if s == 0 else front_all[s - 1]
        at = columns(isub if s == 0 else source("sub", s))
        gw_loc[at, :] = gw_loc[at, :] + dot(plane, fhi, 0, 0)
    gw_loc[L:L + KU, :] = a_gw2[0:KU, 0:L] + a_gw2[KP:KP + KU, L:2 * L]
    gb1 = jnp.sum(front_sum, axis=0, keepdims=True)
    gb2 = jnp.sum(a_gb2[...], axis=1, keepdims=True)
    eye = (lax.broadcasted_iota(jnp.int32, (KU, L), 0) == lax.broadcasted_iota(jnp.int32, (KU, L), 1)).astype(F32)
    gb2_row = jnp.sum(gb2 * eye, axis=0, keepdims=True)
    gw_loc[L + KU:L + KU + 8, :] = jnp.concatenate([gb1, gb2_row, jnp.zeros((6, L), F32)], axis=0)

    hr = (L + KU + 8) // nsub

    def rows_of(i):
        return pl.ds(pl.multiple_of(i * hr, hr), hr)

    cps = [go(gw_loc.at[rows_of(peer("sub", s))], gw_sub.at[s - 1], "sub", s) for s in range(1, nsub)]
    part = gw_loc[rows_of(isub), :]
    for s in range(1, nsub):
        cps[s - 1].wait_recv()
        part = part + gw_sub[s - 1]
    gw_gz[ig] = part
    cps = [go(gw_gz.at[ig], gw_gz.at[ig], "gz", s) for s in range(1, ng)]
    hi, lo = split(a_top[:, rows_y(ig), :].reshape(xs * yb, L) * 0.5)
    otop_ref[...] = dot(jnp.concatenate([hi, lo], axis=1), ww[...], 1, 1).reshape(xs, yb, L)
    ofront_ref[...] = dot(fcat, ww[columns(isub), :], 1, 1)
    for cp in cps:
        cp.wait_recv()
    part = gw_gz[0]
    for j in range(1, ng):
        part = part + gw_gz[j]
    gw_xy[ix] = part * (1.0 / total)
    cps = [go(gw_xy.at[ix], gw_xy.at[ix], "xy", s) for s in range(1, nx)]
    for s in range(1, nsub):
        front_out[s - 1].wait_recv()
        ofront_ref[...] += front_rcv[s - 1]
    for s in range(1, ng):
        top_out[s - 1].wait_recv()
        otop_ref[...] += top_rcv[s - 1].astype(F32)
    for c, s, cp in side_out:
        cp.wait_recv()
        oside_ref[heights(c)] += side_rcv[s - 1, heights(c)].astype(F32)
    for cp in cps:
        cp.wait_recv()
    full = gw_xy[0]
    for j in range(1, nx):
        full = full + gw_xy[j]
    gw_full[rows_of(isub), :] = full
    cps = [go(gw_full.at[rows_of(isub)], gw_full.at[rows_of(isub)], "sub", s) for s in range(1, nsub)]
    for cp in cps:
        cp.wait_recv()
    ogw1_ref[...] = gw_full[0:L, :]
    ogw2_ref[...] = gw_full[L:L + k, :]
    ogb_ref[...] = gw_full[L + KU:L + KU + 8, :]
    for cp in started:
        cp.wait_send()


def on_device(nx, ng, nsub, top, front, side, labels, w_in, b_in, w_out, b_out):
    xs, zs, ys = labels.shape
    total = xs * zs * ys * nx * ng * nsub
    k = w_out.shape[1]
    ns = nx if L // nx >= 16 else 1
    if ns == 1:
        side = lax.all_gather(side, "xy", axis=2, tiled=True)
    cs, cf = L // ns, L // nsub
    bo = jnp.pad(b_out, (0, L - k)).reshape(1, L)
    gr = L + KU + 8
    rows = zs // CHUNKS // 2 * ys
    copies = CHUNKS * (ns - 1) * 2 + (ng - 1) * 3 + (nsub - 1) * 4 + (nx - 1)
    cfg = (ns, nx, ng, nsub, xs, zs, ys, k, total)
    vm = pl.BlockSpec(memory_space=pltpu.VMEM)
    V = pltpu.VMEM
    one = max(ns - 1, 1)
    otop, ofront, oside, ogw1, ogw2, ogb = pl.pallas_call(
        functools.partial(kernel, cfg),
        out_shape=(
            jax.ShapeDtypeStruct(top.shape, F32),
            jax.ShapeDtypeStruct((xs * zs, cf), F32),
            jax.ShapeDtypeStruct((zs, cs, ys), F32),
            jax.ShapeDtypeStruct((L, L), F32),
            jax.ShapeDtypeStruct((k, L), F32),
            jax.ShapeDtypeStruct((8, L), F32),
        ),
        in_specs=[vm] * 8,
        out_specs=(vm,) * 6,
        scratch_shapes=[
            V((ng - 1,) + top.shape, BF16), V((nsub - 1, xs * zs, cf), BF16), V((zs, L, ys), BF16),
            V((2 * KP, 2 * L), BF16), V((2 * L, 2 * KP), BF16), V((L, 2 * L), BF16),
            V((xs, ys, L), F32), V((xs, zs, L), F32), V((zs // CHUNKS, ys, L), F32),
            V((rows, 2 * L), BF16), V((rows, 2 * L), BF16), V((2 * KP, rows), BF16),
            V((zs // CHUNKS, L, ys), F32),
            V((xs, ys, L), F32), V((xs, zs, L), F32), V((zs, ys, L), F32),
            V((2 * KP, 2 * L), F32), V((KU, L), F32),
            V((ng - 1,) + top.shape, BF16), V((ng - 1,) + top.shape, BF16),
            V((nsub - 1, xs * zs, cf), F32), V((nsub - 1, xs * zs, cf), F32),
            V((zs, L, ys), BF16), V((one, zs, cs, ys), BF16),
            V((gr, L), F32), V((nsub - 1, gr // nsub, L), F32),
            V((ng, gr // nsub, L), F32), V((nx, gr // nsub, L), F32), V((gr, L), F32),
            pltpu.SemaphoreType.DMA((copies,)), pltpu.SemaphoreType.DMA((copies,)),
        ],
        compiler_params=pltpu.CompilerParams(
            collective_id=0, has_side_effects=True, vmem_limit_bytes=60 * 1024 * 1024),
    )(top, front.reshape(xs * zs, cf), side.transpose(1, 2, 0), labels, w_in, b_in.reshape(1, L), w_out.T, bo)
    gside = oside.transpose(2, 0, 1)
    if ns == 1:
        gside = lax.psum_scatter(gside, "xy", scatter_dimension=2, tiled=True)
    return (otop, ofront.reshape(front.shape), gside, ogw1, ogb[0], ogw2.T, ogb[1, :k])


def solution(mesh):
    in_specs = (
        P(("groups", "xy"), ("sub", "gz"), None),
        P(("groups", "xy"), "gz", "sub"),
        P(("groups", "sub"), "gz", "xy"),
        P(("groups", "xy"), "gz", "sub"),
        P(),
        P(),
        P(),
        P(),
    )
    out_specs = (
        P(("groups", "xy"), ("sub", "gz"), None),
        P(("groups", "xy"), "gz", "sub"),
        P(("groups", "sub"), "gz", "xy"),
        P("groups", None),
        P("groups"),
        P("groups", None),
        P("groups"),
    )
    body = functools.partial(on_device, mesh.shape["xy"], mesh.shape["gz"], mesh.shape["sub"])
    return jax.shard_map(body, mesh=mesh, in_specs=in_specs, out_specs=out_specs, check_vma=False)
```
